512 devices in a mesh: af: 4 (over x), ga: 8 (over y, core), ha: 16 (over z).
Axes of the slice: x: 4, y: 4, z: 16, core: 2. Of those that a mesh axis runs over, the one named last changes fastest.
Arguments:
- field: float32 [512, 256, 2048], P('af', 'ga', 'ha'), may hold values from -33 to 33, as said below
- start: float32 [512, 64], replicated, may hold values from -6 to 6
Outputs:
- core: float32 [64, 256, 2048], P('af', 'ga', 'ha')
The draws below stay inside these ranges and needn't reach their ends.
Inputs may be any that keep to these rules, and one draw needn't show every extreme that they name: `field`: real values.
All inputs are finite; a program needn't handle non-finite values.
Results may differ from the reference program's by a relative error of at most 0.0003.
Values sent between devices are 32-bit elements; how exact they have to be, the bound alone decides.
A program may use at most 64 MiB of HBM per device.

```python
import jax
import jax.numpy as jnp
from jax import lax

I1 = 512
RANK = 64
I4 = 4
ITERS = 6
I2 = 256
I3 = 512


def draw_field(key, part):
    key = jax.random.fold_in(key, 7)
    keys = jax.random.split(key, 4)
    scales = jnp.exp(jax.random.uniform(keys[0], (I1,), jnp.float32, jnp.log(0.3), jnp.log(3.0)))
    noise = jax.random.truncated_normal(keys[1], -6.0, 6.0, (I1, I2, I3 * I4), jnp.float32)
    weights = jax.random.uniform(keys[2], (3, I1), jnp.float32, -0.8, 0.8)
    shapes = jax.random.truncated_normal(keys[3], -6.0, 6.0, (3, I2, I3 * I4), jnp.float32)
    result = scales[:, None, None] * noise
    for index in range(3):
        result = result + weights[index][:, None, None] * shapes[index][None]
    return result


def bell_draw(stream_key, shape, scale, most, dtype=jnp.bfloat16):
    values = jax.random.normal(stream_key, shape, jnp.float32) * scale
    return jnp.minimum(jnp.maximum(values, -most), most).astype(dtype)


def setup_inputs(seed: int = 0) -> dict:
    key_list = jax.random.split(jax.random.key(seed), 3)
    return {
        "field": draw_field(jax.random.fold_in(key_list[2], 71), 0),
        "start": bell_draw(key_list[1], (I1, RANK), 1.0, 6.0, jnp.float32),
    }


def reference(field, start):
    highest = lax.Precision.HIGHEST
    unfold = field.reshape(I1, -1)
    ncols = unfold.shape[1]
    gram = jnp.dot(unfold.astype(jnp.float32), unfold.T.astype(jnp.float32), precision=highest, preferred_element_type=jnp.float32) * (1.0 / ncols)
    basis = start
    for step in range(ITERS):
        work = jnp.dot(gram.astype(jnp.float32), basis.astype(jnp.float32), precision=highest, preferred_element_type=jnp.float32)
        inner = jnp.dot(work.T.astype(jnp.float32), work.astype(jnp.float32), precision=highest, preferred_element_type=jnp.float32)
        lower = jnp.linalg.cholesky(inner)
        basis = lax.linalg.triangular_solve(lower, work, left_side=False, lower=True, transpose_a=True)
    core = jnp.dot(basis.T.astype(jnp.float32), unfold.astype(jnp.float32), precision=highest, preferred_element_type=jnp.float32)
    return core.reshape(RANK, I2, I3 * I4)
```

```python
import functools

import jax
import jax.numpy as jnp
from jax import lax
from jax.experimental import pallas as pl
from jax.experimental.pallas import tpu as pltpu
from jax.sharding import PartitionSpec as P

ITERS = 6
HIGHEST = lax.Precision.HIGHEST
MESH = pl.DeviceIdType.MESH
VMEM_LIMIT = 56 * 2**20


def dot_nt(a, b):
    dims = (((1,), (1,)), ((), ()))
    return lax.dot_general(a, b, dims, precision=HIGHEST, preferred_element_type=jnp.float32)


def dot(a, b):
    return jnp.dot(a, b, precision=HIGHEST, preferred_element_type=jnp.float32)


def chol_inverse(inner):
    n = inner.shape[0]
    width = 2 * n
    panels = n // 8
    sub = lax.broadcasted_iota(jnp.int32, (8, width), 0)
    lane = lax.broadcasted_iota(jnp.int32, (8, n), 1)
    subn = lax.broadcasted_iota(jnp.int32, (8, n), 0)
    rows = []
    for m in range(panels):
        eye = jnp.where(lane == subn + 8 * m, 1.0, 0.0).astype(jnp.float32)
        rows.append(jnp.concatenate([inner[8 * m:8 * m + 8, :], eye], axis=1))
    full = (8, width)
    out = []
    for k in range(panels):
        cols = {m: [jnp.broadcast_to(rows[m][:, 8 * k + p:8 * k + p + 1], full) for p in range(8)] for m in range(k, panels)}
        D = {}
        for p in range(8):
            for q in range(p, 8):
                D[q, p] = jnp.broadcast_to(cols[k][p][q:q + 1, :], full)
        row = [jnp.broadcast_to(rows[k][p:p + 1, :], full) for p in range(8)]
        dinv = []
        for p in range(8):
            dinv.append(1.0 / D[p, p])
            for q in range(p + 1, 8):
                f = D[q, p] * dinv[p]
                for r in range(p + 1, q + 1):
                    D[q, r] = D[q, r] - f * D[r, p]
                row[q] = row[q] - f * row[p]
                for m in range(k + 1, panels):
                    cols[m][q] = cols[m][q] - f * cols[m][p]
        for m in range(k + 1, panels):
            acc = rows[m]
            for p in range(8):
                acc = acc - (cols[m][p] * dinv[p]) * row[p]
            rows[m] = acc
        res = row[0] * lax.rsqrt(D[0, 0])
        for p in range(1, 8):
            res = jnp.where(sub == p, row[p] * lax.rsqrt(D[p, p]), res)
        out.append(res[:, n:])
    return jnp.concatenate(out, axis=0)


def iterate_kernel(iters, scale, s_ref, start_ref, out_ref, g_ref, w_ref):
    for p in range(4):
        blk = s_ref[pl.ds(128 * p, 128), :] * scale
        g_ref[128 * p:128 * p + 128, 128 * p:128 * p + 128] = blk
        q = (p + 1) % 4
        blk = s_ref[pl.ds(512 + 128 * p, 128), :] * scale
        g_ref[128 * p:128 * p + 128, 128 * q:128 * q + 128] = blk
        g_ref[128 * q:128 * q + 128, 128 * p:128 * p + 128] = blk.T
    for p in range(2):
        q = p + 2
        blk = s_ref[pl.ds(1024 + 128 * p, 128), :] * scale
        g_ref[128 * p:128 * p + 128, 128 * q:128 * q + 128] = blk
        g_ref[128 * q:128 * q + 128, 128 * p:128 * p + 128] = blk.T
    w_ref[...] = dot(start_ref[...].T, g_ref[...])

    def step(i, carry):
        work = w_ref[...]
        linv = chol_inverse(dot_nt(work, work))
        ahead = dot(work, g_ref[...])
        w_ref[...] = dot(linv, ahead)
        return carry
    lax.fori_loop(0, iters - 1, step, 0)
    work = w_ref[...]
    linv = chol_inverse(dot_nt(work, work))
    out_ref[...] = dot(linv, work)


def iterate(s, start, iters, scale):
    n, r = start.shape
    return pl.pallas_call(
        functools.partial(iterate_kernel, iters, scale),
        out_shape=jax.ShapeDtypeStruct((r, n), jnp.float32),
        in_specs=[pl.BlockSpec(memory_space=pltpu.VMEM)] * 2,
        out_specs=pl.BlockSpec(memory_space=pltpu.VMEM),
        scratch_shapes=[pltpu.VMEM((n, n), jnp.float32), pltpu.VMEM((r, n), jnp.float32)],
        compiler_params=pltpu.CompilerParams(vmem_limit_bytes=VMEM_LIMIT),
        name="iterate",
    )(s, start)


def gram_kernel(field_ref, cols_ref, gram_ref, half, near, acc, slots, quad, fours, full,
                in_send, in_recv, own_sem, core_send, core_recv, plane_send, plane_recv,
                z_send, z_recv, out_send, out_recv):
    x, g, z = lax.axis_index("af"), lax.axis_index("ga"), lax.axis_index("ha")
    core = lax.rem(g, 2)
    y = g // 2
    rows = field_ref.shape[0]
    parts = 4
    chunk = rows // parts

    def at(dx, dg, dz):
        return {"af": lax.rem(x + dx, 4), "ga": lax.rem(g + dg, 8), "ha": lax.rem(z + dz, 16)}

    other_core = {"af": x, "ga": g + 1 - 2 * core, "ha": z}
    plane = [(a, b) for a in range(4) for b in range(4) if (a, b) != (0, 0)]

    barrier = pltpu.get_barrier_semaphore()
    partners = [at(0, 0, d) for d in (4, 8, 12, 1, 2, 15, 14)]
    partners += [at(a, 2 * b, 0) for a, b in plane] + [other_core]
    for device in partners:
        pl.semaphore_signal(barrier, inc=1, device_id=device, device_id_type=MESH)
    pl.semaphore_wait(barrier, len(partners))

    sends = []
    for c in range(parts):
        for k, d in enumerate((1, 3, 2)):
            to = lax.rem(x + d, 4)
            copy = pltpu.make_async_remote_copy(
                src_ref=field_ref.at[pl.ds(c * chunk, chunk), pl.ds(to * 8, 8), :],
                dst_ref=cols_ref.at[pl.ds(x * rows + c * chunk, chunk)],
                send_sem=in_send.at[k, c],
                recv_sem=in_recv.at[k, c],
                device_id=at(d, 0, 0),
                device_id_type=MESH,
            )
            copy.start()
            sends.append(copy)
    own = pltpu.make_async_copy(
        field_ref.at[:, pl.ds(x * 8, 8), :], cols_ref.at[pl.ds(x * rows, rows)], own_sem
    )
    own.start()

    def arrived(k, d):
        for c in range(parts):
            source = lax.rem(x + 4 - d, 4)
            landing = cols_ref.at[pl.ds(source * rows + c * chunk, chunk)]
            pltpu.make_async_remote_copy(
                src_ref=landing, dst_ref=landing, send_sem=in_send.at[k, c],
                recv_sem=in_recv.at[k, c], device_id=at(d, 0, 0), device_id_type=MESH,
            ).wait_recv()

    flat = cols_ref.reshape(4 * rows * 8, 128)

    def block(p, q, slot):
        total = jnp.zeros((rows, rows), jnp.float32)
        for s in range(0, 8, 2):
            left = [flat[pl.ds(p * rows * 8 + s + t, rows, stride=8), :] for t in range(2)]
            right = [flat[pl.ds(q * rows * 8 + s + t, rows, stride=8), :] for t in range(2)]
            total += dot_nt(jnp.concatenate(left, axis=1), jnp.concatenate(right, axis=1))
        half[pl.ds(slot * rows, rows), :] = total

    after, opposite, before = (lax.rem(x + d, 4) for d in (1, 2, 3))
    own.wait()
    block(x, x, x)
    arrived(1, 3)
    block(x, after, 4 + x)
    block(after, after, after)
    arrived(0, 1)
    block(before, x, 4 + before)
    block(before, before, before)
    pair = lax.rem(after, 2)
    block(pair, pair + 2, 8 + pair)
    arrived(2, 2)
    block(after, opposite, 4 + after)
    block(opposite, before, 4 + opposite)
    block(opposite, opposite, opposite)
    pair = lax.rem(x, 2)
    block(pair, pair + 2, 8 + pair)

    count = half.shape[0] // 2
    mine = pl.ds(core * count, count)
    swap = pltpu.make_async_remote_copy(
        src_ref=half.at[pl.ds((1 - core) * count, count)], dst_ref=near,
        send_sem=core_send.at[0], recv_sem=core_recv.at[0],
        device_id=other_core, device_id_type=MESH,
    )
    swap.start()
    swap.wait_recv()
    sends.append(swap)
    acc[...] = half[mine, :] + near[...]

    size = count // 16
    me = x * 4 + y
    for i, (a, b) in enumerate(plane):
        to = lax.rem(x + a, 4) * 4 + lax.rem(y + b, 4)
        copy = pltpu.make_async_remote_copy(
            src_ref=acc.at[pl.ds(to * size, size)], dst_ref=slots.at[me],
            send_sem=plane_send.at[i], recv_sem=plane_recv.at[i],
            device_id=at(a, 2 * b, 0), device_id_type=MESH,
        )
        copy.start()
        sends.append(copy)
    slots[me] = acc[pl.ds(me * size, size), :]
    for copy in sends[-15:]:
        copy.wait_recv()
    zq, zr = z // 4, lax.rem(z, 4)
    total = slots[0]
    for i in range(1, 16):
        total += slots[i]
    quad[zq] = total

    for i, d in enumerate((4, 8, 12)):
        copy = pltpu.make_async_remote_copy(
            src_ref=quad.at[zq], dst_ref=quad.at[zq], send_sem=z_send.at[i],
            recv_sem=z_recv.at[i], device_id=at(0, 0, d), device_id_type=MESH,
        )
        copy.start()
        sends.append(copy)
    for copy in sends[-3:]:
        copy.wait_recv()
    fours[zr] = ((quad[0] + quad[1]) + quad[2]) + quad[3]
    for i, d in enumerate((1, 15, 2)):
        copy = pltpu.make_async_remote_copy(
            src_ref=fours.at[zr], dst_ref=fours.at[zr], send_sem=z_send.at[3 + i],
            recv_sem=z_recv.at[3 + i], device_id=at(0, 0, d), device_id_type=MESH,
        )
        copy.start()
        sends.append(copy)
    for copy in sends[-3:]:
        copy.wait_recv()
    total = ((fours[0] + fours[1]) + fours[2]) + fours[3]

    here = pl.ds(core * count + me * size, size)
    full[here, :] = total
    for i, (a, b) in enumerate(plane):
        copy = pltpu.make_async_remote_copy(
            src_ref=full.at[here], dst_ref=full.at[here],
            send_sem=out_send.at[i], recv_sem=out_recv.at[i],
            device_id=at(a, 2 * b, 0), device_id_type=MESH,
        )
        copy.start()
        sends.append(copy)
    for copy in sends[-15:]:
        copy.wait_recv()
    swap = pltpu.make_async_remote_copy(
        src_ref=full.at[mine], dst_ref=full.at[mine],
        send_sem=core_send.at[1], recv_sem=core_recv.at[1],
        device_id=other_core, device_id_type=MESH,
    )
    swap.start()
    swap.wait_recv()
    sends.append(swap)
    gram_ref[...] = full[...]
    for copy in sends:
        copy.wait_send()


def gram_blocks(field):
    rows = field.shape[0]
    dma = pltpu.SemaphoreType.DMA
    vmem = pltpu.VMEM
    return pl.pallas_call(
        gram_kernel,
        out_shape=(
            jax.ShapeDtypeStruct((4 * rows, 8, 128), jnp.float32),
            jax.ShapeDtypeStruct((10 * rows, rows), jnp.float32),
        ),
        in_specs=[pl.BlockSpec(memory_space=pl.ANY)],
        out_specs=(pl.BlockSpec(memory_space=vmem), pl.BlockSpec(memory_space=vmem)),
        scratch_shapes=[
            vmem((10 * rows, rows), jnp.float32),
            vmem((5 * rows, rows), jnp.float32),
            vmem((5 * rows, rows), jnp.float32),
            vmem((16, 5 * rows // 16, rows), jnp.float32),
            vmem((4, 5 * rows // 16, rows), jnp.float32),
            vmem((4, 5 * rows // 16, rows), jnp.float32),
            vmem((10 * rows, rows), jnp.float32),
            dma((3, 4)), dma((3, 4)), dma(()), dma((2,)), dma((2,)), dma((15,)), dma((15,)),
            dma((6,)), dma((6,)), dma((15,)), dma((15,)),
        ],
        compiler_params=pltpu.CompilerParams(
            collective_id=0, has_side_effects=True, vmem_limit_bytes=VMEM_LIMIT
        ),
        name="gram_blocks",
    )(field)


def project_kernel(cols_ref, basis_ref, out_ref, proj, stage, send_sem, recv_sem):
    x = lax.axis_index("af")

    def at(d):
        return {"af": lax.rem(x + d, 4)}

    barrier = pltpu.get_barrier_semaphore()
    for d in (1, 2, 3):
        pl.semaphore_signal(barrier, inc=1, device_id=at(d), device_id_type=MESH)
    ranks, total_rows = basis_ref.shape
    flat = cols_ref.reshape(total_rows * 8, 128)
    flat_out = proj.reshape(ranks * 8, 128)
    basis = basis_ref[...]
    for s in range(0, 8, 2):
        pieces = [flat[pl.ds(s + t, total_rows, stride=8), :] for t in range(2)]
        part = dot(basis, jnp.concatenate(pieces, axis=1))
        for t in range(2):
            flat_out[pl.ds(s + t, ranks, stride=8), :] = part[:, 128 * t:128 * t + 128]
    pl.semaphore_wait(barrier, 3)
    share = ranks // 4
    copies = []
    for k, d in enumerate((2, 1, 3)):
        to = lax.rem(x + d, 4)
        copy = pltpu.make_async_remote_copy(
            src_ref=proj.at[pl.ds(to * share, share)],
            dst_ref=stage.at[:, pl.ds(x * 8, 8), :],
            send_sem=send_sem.at[k], recv_sem=recv_sem.at[k],
            device_id=at(d), device_id_type=MESH,
        )
        copy.start()
        copies.append(copy)
    stage[:, pl.ds(x * 8, 8), :] = proj[pl.ds(x * share, share)]
    for copy in copies:
        copy.wait_recv()
    out_ref[...] = stage[...]
    for copy in copies:
        copy.wait_send()


def project(cols, basis):
    ranks = basis.shape[0]
    dma = pltpu.SemaphoreType.DMA
    vmem = pltpu.VMEM
    return pl.pallas_call(
        project_kernel,
        out_shape=jax.ShapeDtypeStruct((ranks // 4, 32, 128), jnp.float32),
        in_specs=[pl.BlockSpec(memory_space=vmem)] * 2,
        out_specs=pl.BlockSpec(memory_space=vmem),
        scratch_shapes=[
            vmem((ranks, 8, 128), jnp.float32),
            vmem((ranks // 4, 32, 128), jnp.float32),
            dma((3,)), dma((3,)),
        ],
        compiler_params=pltpu.CompilerParams(
            collective_id=1, has_side_effects=True, vmem_limit_bytes=VMEM_LIMIT
        ),
        name="project",
    )(cols, basis)


def per_device(field, start):
    ncols = field.shape[1] * field.shape[2] * lax.axis_size("ga") * lax.axis_size("ha")
    cols, blocks = gram_blocks(field)
    basis = iterate(blocks, start, ITERS, 1.0 / ncols)
    return project(cols, basis)


def solution(mesh):
    placed = (P("af", "ga", "ha"), P())
    return jax.shard_map(
        per_device, mesh=mesh, in_specs=placed, out_specs=P("af", "ga", "ha"), check_vma=False
    )
```

```python
import functools

import jax
import jax.numpy as jnp
from jax import lax
from jax.experimental import pallas as pl
from jax.experimental.pallas import tpu as pltpu
from jax.sharding import PartitionSpec as P

ITERS = 6
HIGHEST = lax.Precision.HIGHEST
MESH = pl.DeviceIdType.MESH
NT = (((1,), (1,)), ((), ()))
VMEM_LIMIT = 56 * 2**20


def dot(a, b):
    return jnp.dot(a, b, precision=HIGHEST, preferred_element_type=jnp.float32)


def dot_nt(a, b):
    return lax.dot_general(a, b, NT, precision=HIGHEST, preferred_element_type=jnp.float32)


def dot16(a, b):
    return jnp.dot(a, b, preferred_element_type=jnp.float32)


def dot16_nt(a, b):
    return lax.dot_general(a, b, NT, preferred_element_type=jnp.float32)


def split(x):
    high = x.astype(jnp.bfloat16)
    rest = x - high.astype(jnp.float32)
    mid = rest.astype(jnp.bfloat16)
    low = (rest - mid.astype(jnp.float32)).astype(jnp.bfloat16)
    return high, mid, low


def chol_inverse(inner):
    n = inner.shape[0]
    width = 2 * n
    panels = n // 8
    sub = lax.broadcasted_iota(jnp.int32, (8, width), 0)
    lane = lax.broadcasted_iota(jnp.int32, (8, n), 1)
    subn = lax.broadcasted_iota(jnp.int32, (8, n), 0)
    rows = []
    for m in range(panels):
        eye = jnp.where(lane == subn + 8 * m, 1.0, 0.0).astype(jnp.float32)
        rows.append(jnp.concatenate([inner[8 * m:8 * m + 8, :], eye], axis=1))
    full = (8, width)
    out = []
    for k in range(panels):
        cols = {m: [jnp.broadcast_to(rows[m][:, 8 * k + p:8 * k + p + 1], full) for p in range(8)] for m in range(k, panels)}
        D = {}
        for p in range(8):
            for q in range(p, 8):
                D[q, p] = jnp.broadcast_to(cols[k][p][q:q + 1, :], full)
        row = [jnp.broadcast_to(rows[k][p:p + 1, :], full) for p in range(8)]
        dinv = []
        for p in range(8):
            dinv.append(1.0 / D[p, p])
            for q in range(p + 1, 8):
                f = D[q, p] * dinv[p]
                for r in range(p + 1, q + 1):
                    D[q, r] = D[q, r] - f * D[r, p]
                row[q] = row[q] - f * row[p]
                for m in range(k + 1, panels):
                    cols[m][q] = cols[m][q] - f * cols[m][p]
        for m in range(k + 1, panels):
            acc = rows[m]
            for p in range(8):
                acc = acc - (cols[m][p] * dinv[p]) * row[p]
            rows[m] = acc
        res = row[0] * lax.rsqrt(D[0, 0])
        for p in range(1, 8):
            res = jnp.where(sub == p, row[p] * lax.rsqrt(D[p, p]), res)
        out.append(res[:, n:])
    return jnp.concatenate(out, axis=0)


def step_kernel(iters, scale, field_ref, start_ref, out_ref, cols, high, mid, low, half, near, acc,
                slots, quad, fours, full, gram, work_ref, proj, stage, in_send, in_recv, own_sem,
                core_send, core_recv, plane_send, plane_recv, z_send, z_recv, back_send, back_recv,
                out_send, out_recv, met):
    x, g, z = lax.axis_index("af"), lax.axis_index("ga"), lax.axis_index("ha")
    core = lax.rem(g, 2)
    y = g // 2
    rows = field_ref.shape[0]

    def at(dx, dg, dz):
        return {"af": lax.rem(x + dx, 4), "ga": lax.rem(g + dg, 8), "ha": lax.rem(z + dz, 16)}

    other_core = {"af": x, "ga": g + 1 - 2 * core, "ha": z}
    plane = [(a, b) for a in range(4) for b in range(4) if (a, b) != (0, 0)]
    sends = []

    def send(src, dst, send_sem, recv_sem, device):
        copy = pltpu.make_async_remote_copy(
            src_ref=src, dst_ref=dst, send_sem=send_sem, recv_sem=recv_sem,
            device_id=device, device_id_type=MESH,
        )
        copy.start()
        sends.append(copy)
        return copy

    barrier = pltpu.get_barrier_semaphore()
    nearest = [at(1, 0, 0), at(3, 0, 0), at(2, 0, 0), other_core]
    nearest += [at(0, 2, 0), at(0, 6, 0), at(0, 0, 1), at(0, 0, 15)]
    for device in nearest:
        pl.semaphore_signal(barrier, inc=1, device_id=device, device_id_type=MESH)
    pl.semaphore_wait(barrier, len(nearest))

    for k, d in enumerate((1, 3, 2)):
        send(
            field_ref.at[:, pl.ds(lax.rem(x + d, 4) * 8, 8), :], cols.at[pl.ds(x * rows, rows)],
            in_send.at[k], in_recv.at[k], at(d, 0, 0),
        )
    incoming = {d: sends[k] for k, d in enumerate((3, 1, 2))}
    own = pltpu.make_async_copy(
        field_ref.at[:, pl.ds(x * 8, 8), :], cols.at[pl.ds(x * rows, rows)], own_sem
    )
    own.start()

    rounds = (
        (at(0, 2, 0), at(0, 6, 0), at(0, 0, 1), at(0, 0, 15)),
        (at(0, 4, 0), at(0, 0, 2), at(0, 0, 14)),
        (at(0, 0, 4), at(0, 0, 12)),
    )
    index = 0
    for devices in rounds:
        for i, device in enumerate(devices):
            pl.semaphore_signal(met.at[index + i], inc=1, device_id=device, device_id_type=MESH)
        for i in range(len(devices)):
            pl.semaphore_wait(met.at[index + i], 1)
        index += len(devices)

    flat = cols.reshape(4 * rows * 8, 128)

    def ready(p):
        for s in range(8):
            parts = split(flat[pl.ds(p * rows * 8 + s, rows, stride=8), :])
            for ref, part in zip((high, mid, low), parts):
                ref[pl.ds(p * rows, rows), 128 * s:128 * s + 128] = part

    def block(p, q, slot):
        left, right = pl.ds(p * rows, rows), pl.ds(q * rows, rows)
        main = dot16_nt(
            jnp.concatenate([high[left, :], mid[left, :]], axis=0),
            jnp.concatenate([high[right, :], mid[right, :]], axis=0),
        )
        small = dot16_nt(low[left, :], high[right, :]) + dot16_nt(high[left, :], low[right, :])
        small += main[rows:, rows:]
        half[pl.ds(slot * rows, rows), :] = main[:rows, :rows] + (
            (main[:rows, rows:] + main[rows:, :rows]) + small
        )

    after, opposite, before = (lax.rem(x + d, 4) for d in (1, 2, 3))
    own.wait()
    ready(x)
    block(x, x, x)
    incoming[1].wait_recv()
    ready(after)
    block(x, after, 4 + x)
    block(after, after, after)
    incoming[3].wait_recv()
    ready(before)
    block(before, x, 4 + before)
    block(before, before, before)
    pair = lax.rem(after, 2)
    block(pair, pair + 2, 8 + pair)
    incoming[2].wait_recv()
    ready(opposite)
    block(after, opposite, 4 + after)
    block(opposite, before, 4 + opposite)
    block(opposite, opposite, opposite)
    pair = lax.rem(x, 2)
    block(pair, pair + 2, 8 + pair)

    count = half.shape[0] // 2
    mine = pl.ds(core * count, count)
    send(
        half.at[pl.ds((1 - core) * count, count)], near, core_send.at[0], core_recv.at[0], other_core
    ).wait_recv()
    acc[...] = half[mine, :] + near[...]

    size = count // 16
    me = x * 4 + y
    arrivals = []
    for i, (a, b) in enumerate(plane):
        to = lax.rem(x + a, 4) * 4 + lax.rem(y + b, 4)
        arrivals.append(send(
            acc.at[pl.ds(to * size, size)], slots.at[me],
            plane_send.at[i], plane_recv.at[i], at(a, 2 * b, 0),
        ))
    slots[me] = acc[pl.ds(me * size, size), :]
    for copy in arrivals:
        copy.wait_recv()
    zq, zr = z // 4, lax.rem(z, 4)
    total = slots[0]
    for i in range(1, 16):
        total += slots[i]

    for index, (ref, own_slot, steps) in enumerate(((quad, zq, (8, 4, 12)), (fours, zr, (2, 1, 15)))):
        ref[own_slot] = total
        arrivals = [
            send(
                ref.at[own_slot], ref.at[own_slot],
                z_send.at[3 * index + i], z_recv.at[3 * index + i], at(0, 0, d),
            )
            for i, d in enumerate(steps)
        ]
        for copy in arrivals:
            copy.wait_recv()
        total = ((ref[0] + ref[1]) + ref[2]) + ref[3]

    here = pl.ds(core * count + me * size, size)
    full[here, :] = total
    arrivals = [
        send(full.at[here], full.at[here], back_send.at[i], back_recv.at[i], at(a, 2 * b, 0))
        for i, (a, b) in enumerate(plane)
    ]
    for copy in arrivals:
        copy.wait_recv()
    send(
        full.at[mine], full.at[mine], core_send.at[1], core_recv.at[1], other_core
    ).wait_recv()
    for p in range(4):
        q = (p + 1) % 4
        gram[rows * p:rows * p + rows, rows * p:rows * p + rows] = (
            full[rows * p:rows * p + rows, :] * scale
        )
        pairs = [(p, q, 4 + p)] + ([(p, p + 2, 8 + p)] if p < 2 else [])
        for a, b, slot in pairs:
            part = full[rows * slot:rows * slot + rows, :] * scale
            gram[rows * a:rows * a + rows, rows * b:rows * b + rows] = part
            gram[rows * b:rows * b + rows, rows * a:rows * a + rows] = part.T

    work_ref[...] = dot(start_ref[...], gram[...])

    def step(i, carry):
        work = work_ref[...]
        inverse = chol_inverse(dot_nt(work, work))
        ahead = dot(work, gram[...])
        work_ref[...] = dot(inverse, jnp.where(i < iters - 1, ahead, work))
        return carry

    lax.fori_loop(0, iters, step, 0)

    parts = split(work_ref[...])
    ranks = work_ref.shape[0]
    main = dot16(jnp.concatenate(parts, axis=0), high[...])
    middle = dot16(jnp.concatenate(parts[:2], axis=0), mid[...])
    small = dot16(parts[0], low[...])
    result = main[:ranks] + (
        (main[ranks:2 * ranks] + middle[:ranks]) + (middle[ranks:] + (main[2 * ranks:] + small))
    )
    flat_out = proj.reshape(ranks * 8, 128)
    for s in range(8):
        flat_out[pl.ds(s, ranks, stride=8), :] = result[:, 128 * s:128 * s + 128]
    share = ranks // 4
    arrivals = [
        send(
            proj.at[pl.ds(lax.rem(x + d, 4) * share, share)], stage.at[:, pl.ds(x * 8, 8), :],
            out_send.at[k], out_recv.at[k], at(d, 0, 0),
        )
        for k, d in enumerate((2, 1, 3))
    ]
    stage[:, pl.ds(x * 8, 8), :] = proj[pl.ds(x * share, share)]
    for copy in arrivals:
        copy.wait_recv()
    out_ref[...] = stage[...]
    for copy in sends:
        copy.wait_send()


def per_device(field, start):
    ncols = field.shape[1] * field.shape[2] * lax.axis_size("ga") * lax.axis_size("ha")
    rows = field.shape[0]
    total, ranks = start.shape
    dma, vmem, f32 = pltpu.SemaphoreType.DMA, pltpu.VMEM, jnp.float32
    piece = 5 * rows // 16
    return pl.pallas_call(
        functools.partial(step_kernel, ITERS, 1.0 / ncols),
        out_shape=jax.ShapeDtypeStruct((ranks // 4, 32, 128), f32),
        in_specs=[pl.BlockSpec(memory_space=pl.ANY), pl.BlockSpec(memory_space=vmem)],
        out_specs=pl.BlockSpec(memory_space=vmem),
        scratch_shapes=[
            vmem((total, 8, 128), f32),
            vmem((total, 1024), jnp.bfloat16),
            vmem((total, 1024), jnp.bfloat16),
            vmem((total, 1024), jnp.bfloat16),
            vmem((10 * rows, rows), f32),
            vmem((5 * rows, rows), f32),
            vmem((5 * rows, rows), f32),
            vmem((16, piece, rows), f32),
            vmem((4, piece, rows), f32),
            vmem((4, piece, rows), f32),
            vmem((10 * rows, rows), f32),
            vmem((total, total), f32),
            vmem((ranks, total), f32),
            vmem((ranks, 8, 128), f32),
            vmem((ranks // 4, 32, 128), f32),
            dma((3,)), dma((3,)), dma(()), dma((2,)), dma((2,)), dma((15,)), dma((15,)),
            dma((6,)), dma((6,)), dma((15,)), dma((15,)), dma((3,)), dma((3,)),
            pltpu.SemaphoreType.REGULAR((9,)),
        ],
        compiler_params=pltpu.CompilerParams(
            collective_id=0, has_side_effects=True, vmem_limit_bytes=VMEM_LIMIT
        ),
        name="hosvd_step",
    )(field, start.T)


def solution(mesh):
    placed = (P("af", "ga", "ha"), P())
    return jax.shard_map(
        per_device, mesh=mesh, in_specs=placed, out_specs=P("af", "ga", "ha"), check_vma=False
    )
```

```python
import functools

import jax
import jax.numpy as jnp
from jax import lax
from jax.experimental import pallas as pl
from jax.experimental.pallas import tpu as pltpu
from jax.sharding import PartitionSpec as P

ITERS = 6
HIGHEST = lax.Precision.HIGHEST
MESH = pl.DeviceIdType.MESH
NT = (((1,), (1,)), ((), ()))
VMEM_LIMIT = 56 * 2**20


def dot(a, b):
    return jnp.dot(a, b, precision=HIGHEST, preferred_element_type=jnp.float32)


def dot_nt(a, b):
    return lax.dot_general(a, b, NT, precision=HIGHEST, preferred_element_type=jnp.float32)


def dot16(a, b):
    return jnp.dot(a, b, preferred_element_type=jnp.float32)


def dot16_nt(a, b):
    return lax.dot_general(a, b, NT, preferred_element_type=jnp.float32)


def split(x):
    high = x.astype(jnp.bfloat16)
    rest = x - high.astype(jnp.float32)
    mid = rest.astype(jnp.bfloat16)
    low = (rest - mid.astype(jnp.float32)).astype(jnp.bfloat16)
    return high, mid, low


def chol_inverse(inner):
    n = inner.shape[0]
    panels = n // 8
    full = (8, 2 * n)
    sub = lax.broadcasted_iota(jnp.int32, full, 0)
    lane = lax.broadcasted_iota(jnp.int32, (8, n), 1)
    rows = []
    for m in range(panels):
        eye = jnp.where(lane == sub[:, :n] + 8 * m, 1.0, 0.0).astype(jnp.float32)
        rows.append(jnp.concatenate([inner[8 * m:8 * m + 8, :], eye], axis=1))

    def over_lanes(m, j):
        return jnp.broadcast_to(rows[m][:, j:j + 1], full)

    def over_rows(value, q):
        return jnp.broadcast_to(value[q:q + 1, :], full)

    out = []
    ahead = {m: [over_lanes(m, p) for p in range(8)] for m in range(2)}
    for k in range(panels):
        later = range(k + 1, panels)
        cols = dict(ahead)
        for m in later:
            if m not in cols:
                cols[m] = [over_lanes(m, 8 * k + p) for p in range(8)]
        early = {
            m: [over_lanes(m, 8 * (k + 1) + j) for j in range(8)]
            for m in range(k + 1, min(k + 3, panels))
        }
        row = [over_rows(rows[k], p) for p in range(8)]
        diag = {(q, p): over_rows(cols[k][p], q) for p in range(8) for q in range(p, 8)}
        inv = []
        for p in range(8):
            inv.append(1.0 / diag[p, p])
            for q in range(p + 1, 8):
                factor = diag[q, p] * inv[p]
                for r in range(p + 1, q + 1):
                    diag[q, r] = diag[q, r] - factor * diag[r, p]
                row[q] = row[q] - factor * row[p]
                for m in later:
                    cols[m][q] = cols[m][q] - factor * cols[m][p]
        scaled = {m: [cols[m][p] * inv[p] for p in range(8)] for m in later}
        ahead = {}
        if k + 1 < panels:
            spread = [[over_rows(cols[k + 1][p], j) for p in range(8)] for j in range(8)]
            for m in early:
                ahead[m] = []
                for j in range(8):
                    value = early[m][j]
                    for p in range(8):
                        value = value - scaled[m][p] * spread[j][p]
                    ahead[m].append(value)
        for m in later:
            terms = [scaled[m][p] * row[p] for p in range(8)]
            while len(terms) > 1:
                terms = [terms[i] + terms[i + 1] for i in range(0, len(terms), 2)]
            rows[m] = rows[m] - terms[0]
        done = row[0] * lax.rsqrt(diag[0, 0])
        for p in range(1, 8):
            done = jnp.where(sub == p, row[p] * lax.rsqrt(diag[p, p]), done)
        out.append(done[:, n:])
    return jnp.concatenate(out, axis=0)


def step_kernel(iters, scale, field_ref, start_ref, out_ref, cols, high, mid, low, half, near, acc,
                slots, quad, fours, full, gram, work_ref, proj, stage, in_send, in_recv, own_sem, start_sem,
                core_send, core_recv, plane_send, plane_recv, z_send, z_recv, back_send, back_recv,
                out_send, out_recv, met):
    x, g, z = lax.axis_index("af"), lax.axis_index("ga"), lax.axis_index("ha")
    core = lax.rem(g, 2)
    y = g // 2
    rows = field_ref.shape[0]

    def at(dx, dg, dz):
        return {"af": lax.rem(x + dx, 4), "ga": lax.rem(g + dg, 8), "ha": lax.rem(z + dz, 16)}

    other_core = {"af": x, "ga": g + 1 - 2 * core, "ha": z}
    plane = [
        (2, 2), (1, 2), (3, 2), (2, 1), (2, 3), (1, 1), (1, 3), (3, 1), (3, 3),
        (2, 0), (0, 2), (1, 0), (3, 0), (0, 1), (0, 3),
    ]
    sends = []

    def send(src, dst, send_sem, recv_sem, device):
        copy = pltpu.make_async_remote_copy(
            src_ref=src, dst_ref=dst, send_sem=send_sem, recv_sem=recv_sem,
            device_id=device, device_id_type=MESH,
        )
        copy.start()
        sends.append(copy)
        return copy

    barrier = pltpu.get_barrier_semaphore()
    nearest = [at(1, 0, 0), at(3, 0, 0), at(2, 0, 0), other_core]
    nearest += [at(0, 2, 0), at(0, 6, 0), at(0, 0, 1), at(0, 0, 15)]
    for device in nearest:
        pl.semaphore_signal(barrier, inc=1, device_id=device, device_id_type=MESH)
    pl.semaphore_wait(barrier, len(nearest))

    for k, d in enumerate((1, 3, 2)):
        send(
            field_ref.at[:, pl.ds(lax.rem(x + d, 4) * 8, 8), :], cols.at[pl.ds(x * rows, rows)],
            in_send.at[k], in_recv.at[k], at(d, 0, 0),
        )
    incoming = {d: sends[k] for k, d in enumerate((3, 1, 2))}
    own = pltpu.make_async_copy(
        field_ref.at[:, pl.ds(x * 8, 8), :], cols.at[pl.ds(x * rows, rows)], own_sem
    )
    own.start()
    first = pltpu.make_async_copy(start_ref, work_ref, start_sem)
    first.start()

    rounds = (
        (at(0, 2, 0), at(0, 6, 0), at(0, 0, 1), at(0, 0, 15)),
        (at(0, 4, 0), at(0, 0, 2), at(0, 0, 14)),
        (at(0, 0, 4), at(0, 0, 12)),
    )
    index = 0
    for devices in rounds:
        for i, device in enumerate(devices):
            pl.semaphore_signal(met.at[index + i], inc=1, device_id=device, device_id_type=MESH)
        for i in range(len(devices)):
            pl.semaphore_wait(met.at[index + i], 1)
        index += len(devices)

    flat = cols.reshape(4 * rows * 8, 128)

    def ready(p):
        for s in range(8):
            parts = split(flat[pl.ds(p * rows * 8 + s, rows, stride=8), :])
            for ref, part in zip((high, mid, low), parts):
                ref[pl.ds(p * rows, rows), 128 * s:128 * s + 128] = part

    part = rows // 2
    swaps, held = [], []

    def block(p, q, slot):
        left, right = pl.ds(p * rows, rows), pl.ds(q * rows, rows)
        main = dot16_nt(
            jnp.concatenate([high[left, :], mid[left, :]], axis=0),
            jnp.concatenate([high[right, :], mid[right, :]], axis=0),
        )
        small = dot16_nt(low[left, :], high[right, :]) + dot16_nt(high[left, :], low[right, :])
        small += main[rows:, rows:]
        half[pl.ds(slot * rows, rows), :] = main[:rows, :rows] + (
            (main[:rows, rows:] + main[rows:, :rows]) + small
        )
        theirs = pl.ds(slot * rows + (1 - core) * part, part)
        index = len(swaps)
        swaps.append(send(
            half.at[theirs], near.at[pl.ds(slot * part, part)],
            core_send.at[index], core_recv.at[index], other_core,
        ))
        held.append(slot)

    after, opposite, before = (lax.rem(x + d, 4) for d in (1, 2, 3))
    own.wait()
    ready(x)
    block(x, x, x)
    incoming[1].wait_recv()
    ready(after)
    block(x, after, 4 + x)
    block(after, after, after)
    incoming[3].wait_recv()
    ready(before)
    block(before, x, 4 + before)
    block(before, before, before)
    pair = lax.rem(after, 2)
    block(pair, pair + 2, 8 + pair)
    incoming[2].wait_recv()
    ready(opposite)
    block(after, opposite, 4 + after)
    block(opposite, before, 4 + opposite)
    block(opposite, opposite, opposite)
    pair = lax.rem(x, 2)
    block(pair, pair + 2, 8 + pair)

    count = half.shape[0] // 2
    for copy, slot in zip(swaps, held):
        copy.wait_recv()
        here = pl.ds(slot * part, part)
        acc[here, :] = half[pl.ds(slot * rows + core * part, part), :] + near[here, :]

    size = count // 16
    me = x * 4 + y
    arrivals = []
    for i, (a, b) in enumerate(plane):
        to = lax.rem(x + a, 4) * 4 + lax.rem(y + b, 4)
        arrivals.append(send(
            acc.at[pl.ds(to * size, size)], slots.at[me],
            plane_send.at[i], plane_recv.at[i], at(a, 2 * b, 0),
        ))
    slots[me] = acc[pl.ds(me * size, size), :]
    for copy in arrivals:
        copy.wait_recv()
    zq, zr = z // 4, lax.rem(z, 4)
    total = slots[0]
    for i in range(1, 16):
        total += slots[i]

    for index, (ref, own_slot, steps) in enumerate(((quad, zq, (8, 4, 12)), (fours, zr, (2, 1, 15)))):
        ref[own_slot] = total
        arrivals = [
            send(
                ref.at[own_slot], ref.at[own_slot],
                z_send.at[3 * index + i], z_recv.at[3 * index + i], at(0, 0, d),
            )
            for i, d in enumerate(steps)
        ]
        for copy in arrivals:
            copy.wait_recv()
        total = ((ref[0] + ref[1]) + ref[2]) + ref[3]

    here = pl.ds(me * size, size)
    full[core, here, :] = total
    arrivals = [
        send(
            full.at[core, here], full.at[core, here],
            back_send.at[i], back_recv.at[i], at(a, 2 * b, 0),
        )
        for i, (a, b) in enumerate(plane)
    ]
    swaps = []
    for i, a in enumerate((0, 1, 3, 2)):
        for copy, (da, _) in zip(arrivals, plane):
            if da == (4 - a) % 4:
                copy.wait_recv()
        group = pl.ds(lax.rem(x + a, 4) * 4 * size, 4 * size)
        swaps.append(send(
            full.at[core, group], full.at[core, group],
            core_send.at[10 + i], core_recv.at[10 + i], other_core,
        ))
    for copy in swaps:
        copy.wait_recv()
    pairs = [(p, p, p) for p in range(4)] + [(p, (p + 1) % 4, 4 + p) for p in range(4)]
    pairs += [(p, p + 2, 8 + p) for p in range(2)]
    for a, b, slot in pairs:
        piece = full[:, part * slot:part * slot + part, :].reshape(rows, rows) * scale
        gram[rows * a:rows * a + rows, rows * b:rows * b + rows] = piece
        if a != b:
            gram[rows * b:rows * b + rows, rows * a:rows * a + rows] = piece.T

    first.wait()
    work_ref[...] = dot(work_ref[...], gram[...])

    def step(i, carry):
        work = work_ref[...]
        inverse = chol_inverse(dot_nt(work, work))
        ahead = dot(work, gram[...])
        work_ref[...] = dot(inverse, jnp.where(i < iters - 1, ahead, work))
        return carry

    lax.fori_loop(0, iters, step, 0)

    parts = split(work_ref[...])
    ranks = work_ref.shape[0]
    share = ranks // 4
    flat_out = proj.reshape(ranks * 8, 128)
    arrivals = []
    for h in range(2):
        wide = slice(512 * h, 512 * h + 512)
        main = dot16(jnp.concatenate(parts, axis=0), high[:, wide])
        middle = dot16(jnp.concatenate(parts[:2], axis=0), mid[:, wide])
        small = dot16(parts[0], low[:, wide])
        result = main[:ranks] + (
            (main[ranks:2 * ranks] + middle[:ranks]) + (middle[ranks:] + (main[2 * ranks:] + small))
        )
        for s in range(4):
            flat_out[pl.ds(4 * h + s, ranks, stride=8), :] = result[:, 128 * s:128 * s + 128]
        for k, d in enumerate((2, 1, 3)):
            arrivals.append(send(
                proj.at[pl.ds(lax.rem(x + d, 4) * share, share), pl.ds(4 * h, 4), :],
                stage.at[:, pl.ds(x * 8 + 4 * h, 4), :],
                out_send.at[h, k], out_recv.at[h, k], at(d, 0, 0),
            ))
    stage[:, pl.ds(x * 8, 8), :] = proj[pl.ds(x * share, share)]
    for copy in arrivals:
        copy.wait_recv()
    out_ref[...] = stage[...]
    for copy in sends:
        copy.wait_send()


def per_device(field, start):
    ncols = field.shape[1] * field.shape[2] * lax.axis_size("ga") * lax.axis_size("ha")
    rows = field.shape[0]
    total, ranks = start.shape
    dma, vmem, f32 = pltpu.SemaphoreType.DMA, pltpu.VMEM, jnp.float32
    piece = 5 * rows // 16
    return pl.pallas_call(
        functools.partial(step_kernel, ITERS, 1.0 / ncols),
        out_shape=jax.ShapeDtypeStruct((ranks // 4, 32, 128), f32),
        in_specs=[pl.BlockSpec(memory_space=pl.ANY)] * 2,
        out_specs=pl.BlockSpec(memory_space=vmem),
        scratch_shapes=[
            vmem((total, 8, 128), f32),
            vmem((total, 1024), jnp.bfloat16),
            vmem((total, 1024), jnp.bfloat16),
            vmem((total, 1024), jnp.bfloat16),
            vmem((10 * rows, rows), f32),
            vmem((5 * rows, rows), f32),
            vmem((5 * rows, rows), f32),
            vmem((16, piece, rows), f32),
            vmem((4, piece, rows), f32),
            vmem((4, piece, rows), f32),
            vmem((2, 5 * rows, rows), f32),
            vmem((total, total), f32),
            vmem((ranks, total), f32),
            vmem((ranks, 8, 128), f32),
            vmem((ranks // 4, 32, 128), f32),
            dma((3,)), dma((3,)), dma(()), dma(()), dma((14,)), dma((14,)), dma((15,)), dma((15,)),
            dma((6,)), dma((6,)), dma((15,)), dma((15,)), dma((2, 3)), dma((2, 3)),
            pltpu.SemaphoreType.REGULAR((9,)),
        ],
        compiler_params=pltpu.CompilerParams(
            collective_id=0, has_side_effects=True, vmem_limit_bytes=VMEM_LIMIT
        ),
        name="hosvd_step",
    )(field, start.T)


def solution(mesh):
    placed = (P("af", "ga", "ha"), P())
    return jax.shard_map(
        per_device, mesh=mesh, in_specs=placed, out_specs=P("af", "ga", "ha"), check_vma=False
    )
```

```python
import functools

import jax
import jax.numpy as jnp
from jax import lax
from jax.experimental import pallas as pl
from jax.experimental.pallas import tpu as pltpu
from jax.sharding import PartitionSpec as P

ITERS = 6
HIGHEST = lax.Precision.HIGHEST
MESH = pl.DeviceIdType.MESH
NT = (((1,), (1,)), ((), ()))
VMEM_LIMIT = 32 * 2**20


def dot_nt(a, b):
    return lax.dot_general(a, b, NT, precision=HIGHEST, preferred_element_type=jnp.float32)


def dot16(a, b):
    return jnp.dot(a, b, preferred_element_type=jnp.float32)


def dot16_nt(a, b):
    return lax.dot_general(a, b, NT, preferred_element_type=jnp.float32)


def split(x):
    high = x.astype(jnp.bfloat16)
    rest = x - high.astype(jnp.float32)
    mid = rest.astype(jnp.bfloat16)
    low = (rest - mid.astype(jnp.float32)).astype(jnp.bfloat16)
    return high, mid, low


def times(parts, high, mid, low):
    n = parts[0].shape[0]
    first = dot16(jnp.concatenate(parts, axis=0), high)
    second = dot16(jnp.concatenate(parts[:2], axis=0), mid)
    third = dot16(parts[0], low)
    return first[:n] + (
        (first[n:2 * n] + second[:n]) + (second[n:] + (first[2 * n:] + third))
    )


def wide_times(a, b):
    ah, am, al = split(a)
    zero = jnp.zeros(b.shape, jnp.bfloat16)
    bh, bm, bl = (jnp.concatenate([zero, term], axis=0) for term in split(b))
    left = jnp.concatenate([ah, ah, ah, am, am, al], axis=1)
    return dot16(left, jnp.concatenate([bh, bm, bl, bh, bm, bh], axis=0))


def chol_inverse(inner):
    n = inner.shape[0]
    panels = n // 8
    full = (8, 2 * n)
    sub = lax.broadcasted_iota(jnp.int32, full, 0)
    lane = lax.broadcasted_iota(jnp.int32, full, 1)
    rows = []
    for m in range(panels):
        eye = jnp.where(lane[:, :n] == sub[:, :n] + 8 * m, 1.0, 0.0).astype(jnp.float32)
        rows.append(jnp.concatenate([inner[8 * m:8 * m + 8, :], eye], axis=1))

    def over_lanes(m, j):
        return jnp.broadcast_to(rows[m][:, j:j + 1], full)

    def over_rows(value, q):
        return jnp.broadcast_to(value[q:q + 1, :], full)

    out = []
    ahead = {m: [over_lanes(m, p) for p in range(8)] for m in range(2)}
    for k in range(panels):
        later = range(k + 1, panels)
        cols = dict(ahead)
        for m in later:
            if m not in cols:
                cols[m] = [over_lanes(m, 8 * k + p) for p in range(8)]
        early = {
            m: [over_lanes(m, 8 * (k + 1) + j) for j in range(8)]
            for m in range(k + 1, min(k + 3, panels))
        }
        row = [over_rows(rows[k], p) for p in range(8)]
        diag = {(q, p): over_rows(cols[k][p], q) for p in range(8) for q in range(p, 8)}
        inv = []
        for p in range(8):
            inv.append(1.0 / diag[p, p])
            for q in range(p + 1, 8):
                factor = diag[q, p] * inv[p]
                for r in range(p + 1, q + 1):
                    diag[q, r] = diag[q, r] - factor * diag[r, p]
                row[q] = row[q] - factor * row[p]
                for m in later:
                    cols[m][q] = cols[m][q] - factor * cols[m][p]
        scaled = {m: [cols[m][p] * inv[p] for p in range(8)] for m in later}
        ahead = {}
        if k + 1 < panels:
            spread = [[over_rows(cols[k + 1][p], j) for p in range(8)] for j in range(8)]
            for m in early:
                ahead[m] = []
                for j in range(8):
                    value = early[m][j]
                    for p in range(8):
                        value = value - scaled[m][p] * spread[j][p]
                    ahead[m].append(value)
        for m in later:
            terms = [scaled[m][p] * row[p] for p in range(8)]
            while len(terms) > 1:
                terms = [terms[i] + terms[i + 1] for i in range(0, len(terms), 2)]
            rows[m] = rows[m] - terms[0]
        done = row[0] * lax.rsqrt(diag[0, 0])
        for p in range(1, 8):
            done = jnp.where(sub == p, row[p] * lax.rsqrt(diag[p, p]), done)
        out.append(jnp.where(lane >= n, done, 0.0))
    return jnp.concatenate(out, axis=0)


def step_kernel(iters, scale, field_ref, start_ref, out_ref, cols, high, mid, low, half, near, acc,
                slots, quad, fours, full, gram, gram_mid, gram_low, work_ref, proj, stage, in_send, in_recv, own_sem, start_sem,
                core_send, core_recv, plane_send, plane_recv, z_send, z_recv, back_send, back_recv,
                out_send, out_recv, met):
    x, g, z = lax.axis_index("af"), lax.axis_index("ga"), lax.axis_index("ha")
    core = lax.rem(g, 2)
    y = g // 2
    rows = field_ref.shape[0]

    def at(dx, dg, dz):
        return {"af": lax.rem(x + dx, 4), "ga": lax.rem(g + dg, 8), "ha": lax.rem(z + dz, 16)}

    other_core = {"af": x, "ga": g + 1 - 2 * core, "ha": z}
    plane = [
        (2, 2), (1, 2), (3, 2), (2, 1), (2, 3), (1, 1), (1, 3), (3, 1), (3, 3),
        (2, 0), (0, 2), (1, 0), (3, 0), (0, 1), (0, 3),
    ]
    sends = []

    def send(src, dst, send_sem, recv_sem, device):
        copy = pltpu.make_async_remote_copy(
            src_ref=src, dst_ref=dst, send_sem=send_sem, recv_sem=recv_sem,
            device_id=device, device_id_type=MESH,
        )
        copy.start()
        sends.append(copy)
        return copy

    barrier = pltpu.get_barrier_semaphore()
    nearest = [at(1, 0, 0), at(3, 0, 0), at(2, 0, 0), other_core]
    nearest += [at(0, 2, 0), at(0, 6, 0), at(0, 0, 1), at(0, 0, 15)]
    for device in nearest:
        pl.semaphore_signal(barrier, inc=1, device_id=device, device_id_type=MESH)
    pl.semaphore_wait(barrier, len(nearest))

    for k, d in enumerate((1, 3)):
        send(
            field_ref.at[:, pl.ds(lax.rem(x + d, 4) * 8, 8), :], cols.at[pl.ds(x * rows, rows)],
            in_send.at[k], in_recv.at[k], at(d, 0, 0),
        )
    from_before, from_after = sends

    def send_opposite():
        to = lax.rem(x + 2, 4)
        return [
            send(
                field_ref.at[:, pl.ds(to * 8 + 4 * h, 4), :],
                cols.at[pl.ds(x * rows, rows), pl.ds(4 * h, 4), :],
                in_send.at[2 + h], in_recv.at[2 + h], at(2, 0, 0),
            )
            for h in range(2)
        ]

    from_opposite = send_opposite()
    own = pltpu.make_async_copy(
        field_ref.at[:, pl.ds(x * 8, 8), :], cols.at[pl.ds(x * rows, rows)], own_sem
    )
    own.start()
    first = pltpu.make_async_copy(start_ref, work_ref, start_sem)
    first.start()

    rounds = (
        (at(0, 2, 0), at(0, 6, 0), at(0, 0, 1), at(0, 0, 15)),
        (at(0, 4, 0), at(0, 0, 2), at(0, 0, 14)),
        (at(0, 0, 4), at(0, 0, 12)),
    )
    index = 0
    for turn, devices in enumerate(rounds):
        for i, device in enumerate(devices):
            pl.semaphore_signal(met.at[index + i], inc=1, device_id=device, device_id_type=MESH)
        for i in range(len(devices)):
            pl.semaphore_wait(met.at[index + i], 1)
        index += len(devices)

    flat = cols.reshape(4 * rows * 8, 128)

    def ready(p, start=0, stop=8):
        for s in range(start, stop):
            parts = split(flat[pl.ds(p * rows * 8 + s, rows, stride=8), :])
            for ref, part in zip((high, mid, low), parts):
                ref[pl.ds(p * rows, rows), 128 * s:128 * s + 128] = part

    part = rows // 2
    swaps, held = [], []

    def block(p, q, slot, begin=0, end=8):
        left, right = pl.ds(p * rows, rows), pl.ds(q * rows, rows)
        wide = slice(128 * begin, 128 * end)
        main = dot16_nt(
            jnp.concatenate([high[left, wide], mid[left, wide]], axis=0),
            jnp.concatenate([high[right, wide], mid[right, wide]], axis=0),
        )
        small = dot16_nt(low[left, wide], high[right, wide])
        small += dot16_nt(high[left, wide], low[right, wide]) + main[rows:, rows:]
        total = main[:rows, :rows] + ((main[:rows, rows:] + main[rows:, :rows]) + small)
        whole = pl.ds(slot * rows, rows)
        half[whole, :] = total if begin == 0 else half[whole, :] + total
        if end < 8:
            return
        theirs = pl.ds(slot * rows + (1 - core) * part, part)
        index = len(swaps)
        swaps.append(send(
            half.at[theirs], near.at[pl.ds(slot * part, part)],
            core_send.at[index], core_recv.at[index], other_core,
        ))
        held.append(slot)

    after, opposite, before = (lax.rem(x + d, 4) for d in (1, 2, 3))
    own.wait()
    ready(x)
    block(x, x, x)
    from_after.wait_recv()
    ready(after)
    block(x, after, 4 + x)
    block(after, after, after)
    from_before.wait_recv()
    ready(before)
    block(before, x, 4 + before)
    block(before, before, before)
    pair = lax.rem(after, 2)
    block(pair, pair + 2, 8 + pair)
    for h, copy in enumerate(from_opposite):
        copy.wait_recv()
        begin, end = 4 * h, 4 * h + 4
        ready(opposite, begin, end)
        block(after, opposite, 4 + after, begin, end)
        block(opposite, before, 4 + opposite, begin, end)
        block(opposite, opposite, opposite, begin, end)
        pair = lax.rem(x, 2)
        block(pair, pair + 2, 8 + pair, begin, end)

    count = half.shape[0] // 2
    for copy, slot in zip(swaps, held):
        copy.wait_recv()
        here = pl.ds(slot * part, part)
        acc[here, :] = half[pl.ds(slot * rows + core * part, part), :] + near[here, :]

    size = count // 16
    me = x * 4 + y
    arrivals = []
    for i, (a, b) in enumerate(plane):
        to = lax.rem(x + a, 4) * 4 + lax.rem(y + b, 4)
        arrivals.append(send(
            acc.at[pl.ds(to * size, size)], slots.at[me],
            plane_send.at[i], plane_recv.at[i], at(a, 2 * b, 0),
        ))
    slots[me] = acc[pl.ds(me * size, size), :]
    for copy in arrivals:
        copy.wait_recv()
    zq, zr = z // 4, lax.rem(z, 4)
    total = slots[0]
    for i in range(1, 16):
        total += slots[i]

    for index, (ref, own_slot, steps) in enumerate(((quad, zq, (8, 4, 12)), (fours, zr, (2, 1, 15)))):
        ref[own_slot] = total
        arrivals = [
            send(
                ref.at[own_slot], ref.at[own_slot],
                z_send.at[3 * index + i], z_recv.at[3 * index + i], at(0, 0, d),
            )
            for i, d in enumerate(steps)
        ]
        for copy in arrivals:
            copy.wait_recv()
        total = ((ref[0] + ref[1]) + ref[2]) + ref[3]

    here = pl.ds(me * size, size)
    full[core, here, :] = total
    arrivals = [
        send(
            full.at[core, here], full.at[core, here],
            back_send.at[i], back_recv.at[i], at(a, 2 * b, 0),
        )
        for i, (a, b) in enumerate(plane)
    ]
    swaps = []
    for i, a in enumerate((0, 1, 3, 2)):
        for copy, (da, _) in zip(arrivals, plane):
            if da == (4 - a) % 4:
                copy.wait_recv()
        group = pl.ds(lax.rem(x + a, 4) * 4 * size, 4 * size)
        swaps.append(send(
            full.at[core, group], full.at[core, group],
            core_send.at[10 + i], core_recv.at[10 + i], other_core,
        ))
    for copy in swaps:
        copy.wait_recv()
    pairs = [(p, p, p) for p in range(4)] + [(p, (p + 1) % 4, 4 + p) for p in range(4)]
    pairs += [(p, p + 2, 8 + p) for p in range(2)]
    for a, b, slot in pairs:
        piece = full[:, part * slot:part * slot + part, :].reshape(rows, rows) * scale
        for p, q, value in ((a, b, piece),) if a == b else ((a, b, piece), (b, a, piece.T)):
            for ref, term in zip((gram, gram_mid, gram_low), split(value)):
                ref[rows * p:rows * p + rows, rows * q:rows * q + rows] = term

    first.wait()
    work_ref[...] = times(split(work_ref[...]), gram[...], gram_mid[...], gram_low[...])

    def step(i, carry):
        work = work_ref[...]
        inverse = chol_inverse(dot_nt(work, work))
        ahead = times(split(work), gram[...], gram_mid[...], gram_low[...])
        work_ref[...] = wide_times(inverse, jnp.where(i < iters - 1, ahead, work))
        return carry

    lax.fori_loop(0, iters, step, 0)

    parts = split(work_ref[...])
    ranks = work_ref.shape[0]
    share = ranks // 4
    flat_out = proj.reshape(ranks * 8, 128)
    arrivals = []
    for h in range(2):
        wide = slice(512 * h, 512 * h + 512)
        result = times(parts, high[:, wide], mid[:, wide], low[:, wide])
        for s in range(4):
            flat_out[pl.ds(4 * h + s, ranks, stride=8), :] = result[:, 128 * s:128 * s + 128]
        for k, d in enumerate((2, 1, 3)):
            arrivals.append(send(
                proj.at[pl.ds(lax.rem(x + d, 4) * share, share), pl.ds(4 * h, 4), :],
                stage.at[:, pl.ds(x * 8 + 4 * h, 4), :],
                out_send.at[h, k], out_recv.at[h, k], at(d, 0, 0),
            ))
    stage[:, pl.ds(x * 8, 8), :] = proj[pl.ds(x * share, share)]
    for copy in arrivals:
        copy.wait_recv()
    out_ref[...] = stage[...]
    for copy in sends:
        copy.wait_send()


def per_device(field, start):
    ncols = field.shape[1] * field.shape[2] * lax.axis_size("ga") * lax.axis_size("ha")
    rows = field.shape[0]
    total, ranks = start.shape
    dma, vmem, f32 = pltpu.SemaphoreType.DMA, pltpu.VMEM, jnp.float32
    piece = 5 * rows // 16
    return pl.pallas_call(
        functools.partial(step_kernel, ITERS, 1.0 / ncols),
        out_shape=jax.ShapeDtypeStruct((ranks // 4, 32, 128), f32),
        in_specs=[pl.BlockSpec(memory_space=pltpu.HBM)] * 2,
        out_specs=pl.BlockSpec(memory_space=vmem),
        scratch_shapes=[
            vmem((total, 8, 128), f32),
            vmem((total, 1024), jnp.bfloat16),
            vmem((total, 1024), jnp.bfloat16),
            vmem((total, 1024), jnp.bfloat16),
            vmem((10 * rows, rows), f32),
            vmem((5 * rows, rows), f32),
            vmem((5 * rows, rows), f32),
            vmem((16, piece, rows), f32),
            vmem((4, piece, rows), f32),
            vmem((4, piece, rows), f32),
            vmem((2, 5 * rows, rows), f32),
            vmem((total, total), jnp.bfloat16),
            vmem((total, total), jnp.bfloat16),
            vmem((total, total), jnp.bfloat16),
            vmem((ranks, total), f32),
            vmem((ranks, 8, 128), f32),
            vmem((ranks // 4, 32, 128), f32),
            dma((4,)), dma((4,)), dma(()), dma(()), dma((14,)), dma((14,)), dma((15,)), dma((15,)),
            dma((6,)), dma((6,)), dma((15,)), dma((15,)), dma((2, 3)), dma((2, 3)),
            pltpu.SemaphoreType.REGULAR((9,)),
        ],
        compiler_params=pltpu.CompilerParams(
            collective_id=0, has_side_effects=True, vmem_limit_bytes=VMEM_LIMIT
        ),
        name="hosvd_step",
    )(
        pltpu.with_memory_space_constraint(field, pltpu.HBM),
        pltpu.with_memory_space_constraint(start.T, pltpu.HBM),
    )


def solution(mesh):
    placed = (P("af", "ga", "ha"), P())
    return jax.shard_map(
        per_device, mesh=mesh, in_specs=placed, out_specs=P("af", "ga", "ha"), check_vma=False
    )
```

```python
import functools

import jax
import jax.numpy as jnp
from jax import lax
from jax.experimental import pallas as pl
from jax.experimental.pallas import tpu as pltpu
from jax.sharding import PartitionSpec as P

ITERS = 6
HIGHEST = lax.Precision.HIGHEST
MESH = pl.DeviceIdType.MESH
NT = (((1,), (1,)), ((), ()))
VMEM_LIMIT = 32 * 2**20


def dot_nt(a, b):
    return lax.dot_general(a, b, NT, precision=HIGHEST, preferred_element_type=jnp.float32)


def dot16(a, b):
    return jnp.dot(a, b, preferred_element_type=jnp.float32)


def dot16_nt(a, b):
    return lax.dot_general(a, b, NT, preferred_element_type=jnp.float32)


def split(x):
    high = x.astype(jnp.bfloat16)
    rest = x - high.astype(jnp.float32)
    mid = rest.astype(jnp.bfloat16)
    low = (rest - mid.astype(jnp.float32)).astype(jnp.bfloat16)
    return high, mid, low


def times(parts, high, mid, low):
    n = parts[0].shape[0]
    first = dot16(jnp.concatenate(parts, axis=0), high)
    second = dot16(jnp.concatenate(parts[:2], axis=0), mid)
    third = dot16(parts[0], low)
    return first[:n] + (
        (first[n:2 * n] + second[:n]) + (second[n:] + (first[2 * n:] + third))
    )


def wide_times(a, b):
    ah, am, al = split(a)
    zero = jnp.zeros(b.shape, jnp.bfloat16)
    bh, bm, bl = (jnp.concatenate([zero, term], axis=0) for term in split(b))
    left = jnp.concatenate([ah, ah, ah, am, am, al], axis=1)
    return dot16(left, jnp.concatenate([bh, bm, bl, bh, bm, bh], axis=0))


def chol_inverse(inner):
    n = inner.shape[0]
    panels = n // 8
    full = (8, 2 * n)
    sub = lax.broadcasted_iota(jnp.int32, full, 0)
    lane = lax.broadcasted_iota(jnp.int32, full, 1)
    rows = []
    for m in range(panels):
        eye = jnp.where(lane[:, :n] == sub[:, :n] + 8 * m, 1.0, 0.0).astype(jnp.float32)
        rows.append(jnp.concatenate([inner[8 * m:8 * m + 8, :], eye], axis=1))

    def over_lanes(m, j):
        return jnp.broadcast_to(rows[m][:, j:j + 1], full)

    def over_rows(value, q):
        return jnp.broadcast_to(value[q:q + 1, :], full)

    out = []
    ahead = {m: [over_lanes(m, p) for p in range(8)] for m in range(2)}
    for k in range(panels):
        later = range(k + 1, panels)
        cols = dict(ahead)
        for m in later:
            if m not in cols:
                cols[m] = [over_lanes(m, 8 * k + p) for p in range(8)]
        early = {
            m: [over_lanes(m, 8 * (k + 1) + j) for j in range(8)]
            for m in range(k + 1, min(k + 3, panels))
        }
        row = [over_rows(rows[k], p) for p in range(8)]
        diag = {(q, p): over_rows(cols[k][p], q) for p in range(8) for q in range(p, 8)}
        inv = []
        for p in range(8):
            inv.append(1.0 / diag[p, p])
            for q in range(p + 1, 8):
                factor = diag[q, p] * inv[p]
                for r in range(p + 1, q + 1):
                    diag[q, r] = diag[q, r] - factor * diag[r, p]
                row[q] = row[q] - factor * row[p]
                for m in later:
                    cols[m][q] = cols[m][q] - factor * cols[m][p]
        scaled = {m: [cols[m][p] * inv[p] for p in range(8)] for m in later}
        ahead = {}
        if k + 1 < panels:
            spread = [[over_rows(cols[k + 1][p], j) for p in range(8)] for j in range(8)]
            for m in early:
                ahead[m] = []
                for j in range(8):
                    value = early[m][j]
                    for p in range(8):
                        value = value - scaled[m][p] * spread[j][p]
                    ahead[m].append(value)
        for m in later:
            terms = [scaled[m][p] * row[p] for p in range(8)]
            while len(terms) > 1:
                terms = [terms[i] + terms[i + 1] for i in range(0, len(terms), 2)]
            rows[m] = rows[m] - terms[0]
        done = row[0] * lax.rsqrt(diag[0, 0])
        for p in range(1, 8):
            done = jnp.where(sub == p, row[p] * lax.rsqrt(diag[p, p]), done)
        out.append(jnp.where(lane >= n, done, 0.0))
    return jnp.concatenate(out, axis=0)


def step_kernel(iters, scale, field_ref, start_ref, out_ref, cols, high, mid, low, half, near, acc,
                slots, quad, fours, full, gram, gram_mid, gram_low, work_ref, proj, in_send, in_recv, own_sem, start_sem,
                core_send, core_recv, plane_send, plane_recv, z_send, z_recv, back_send, back_recv,
                out_send, out_recv, met):
    x, g, z = lax.axis_index("af"), lax.axis_index("ga"), lax.axis_index("ha")
    core = lax.rem(g, 2)
    y = g // 2
    rows = field_ref.shape[0]

    def at(dx, dg, dz):
        return {"af": lax.rem(x + dx, 4), "ga": lax.rem(g + dg, 8), "ha": lax.rem(z + dz, 16)}

    other_core = {"af": x, "ga": g + 1 - 2 * core, "ha": z}
    plane = [
        (2, 2), (1, 2), (3, 2), (2, 1), (2, 3), (1, 1), (1, 3), (3, 1), (3, 3),
        (2, 0), (0, 2), (1, 0), (3, 0), (0, 1), (0, 3),
    ]
    sends = []

    def send(src, dst, send_sem, recv_sem, device):
        copy = pltpu.make_async_remote_copy(
            src_ref=src, dst_ref=dst, send_sem=send_sem, recv_sem=recv_sem,
            device_id=device, device_id_type=MESH,
        )
        copy.start()
        sends.append(copy)
        return copy

    barrier = pltpu.get_barrier_semaphore()
    nearest = [at(1, 0, 0), at(3, 0, 0), at(2, 0, 0), other_core]
    nearest += [at(0, 2, 0), at(0, 6, 0), at(0, 0, 1), at(0, 0, 15)]
    for device in nearest:
        pl.semaphore_signal(barrier, inc=1, device_id=device, device_id_type=MESH)
    pl.semaphore_wait(barrier, len(nearest))

    for k, d in enumerate((1, 3)):
        send(
            field_ref.at[:, pl.ds(lax.rem(x + d, 4) * 8, 8), :], cols.at[pl.ds(x * rows, rows)],
            in_send.at[k], in_recv.at[k], at(d, 0, 0),
        )
    from_before, from_after = sends

    def send_opposite():
        to = lax.rem(x + 2, 4)
        return [
            send(
                field_ref.at[:, pl.ds(to * 8 + 2 * h, 2), :],
                cols.at[pl.ds(x * rows, rows), pl.ds(2 * h, 2), :],
                in_send.at[2 + h], in_recv.at[2 + h], at(2, 0, 0),
            )
            for h in range(4)
        ]

    from_opposite = send_opposite()
    own = pltpu.make_async_copy(
        field_ref.at[:, pl.ds(x * 8, 8), :], cols.at[pl.ds(x * rows, rows)], own_sem
    )
    own.start()
    first = pltpu.make_async_copy(start_ref, work_ref, start_sem)
    first.start()

    rounds = (
        (at(0, 2, 0), at(0, 6, 0), at(0, 0, 1), at(0, 0, 15)),
        (at(0, 4, 0), at(0, 0, 2), at(0, 0, 14)),
        (at(0, 0, 4), at(0, 0, 12)),
    )
    index = 0
    for turn, devices in enumerate(rounds):
        for i, device in enumerate(devices):
            pl.semaphore_signal(met.at[index + i], inc=1, device_id=device, device_id_type=MESH)
        for i in range(len(devices)):
            pl.semaphore_wait(met.at[index + i], 1)
        index += len(devices)

    flat = cols.reshape(4 * rows * 8, 128)

    def ready(p, start=0, stop=8):
        for s in range(start, stop):
            parts = split(flat[pl.ds(p * rows * 8 + s, rows, stride=8), :])
            for ref, part in zip((high, mid, low), parts):
                ref[pl.ds(p * rows, rows), 128 * s:128 * s + 128] = part

    part = rows // 2
    swaps, held = [], []

    def block(p, q, slot, begin=0, end=8):
        left, right = pl.ds(p * rows, rows), pl.ds(q * rows, rows)
        wide = slice(128 * begin, 128 * end)
        main = dot16_nt(
            jnp.concatenate([high[left, wide], mid[left, wide]], axis=0),
            jnp.concatenate([high[right, wide], mid[right, wide]], axis=0),
        )
        small = dot16_nt(low[left, wide], high[right, wide])
        small += dot16_nt(high[left, wide], low[right, wide]) + main[rows:, rows:]
        total = main[:rows, :rows] + ((main[:rows, rows:] + main[rows:, :rows]) + small)
        whole = pl.ds(slot * rows, rows)
        half[whole, :] = total if begin == 0 else half[whole, :] + total
        if end < 8:
            return
        theirs = pl.ds(slot * rows + (1 - core) * part, part)
        index = len(swaps)
        swaps.append(send(
            half.at[theirs], near.at[pl.ds(slot * part, part)],
            core_send.at[index], core_recv.at[index], other_core,
        ))
        held.append(slot)

    after, opposite, before = (lax.rem(x + d, 4) for d in (1, 2, 3))
    own.wait()
    ready(x)
    block(x, x, x)
    from_after.wait_recv()
    ready(after)
    block(x, after, 4 + x)
    block(after, after, after)
    from_before.wait_recv()
    ready(before)
    block(before, x, 4 + before)
    block(before, before, before)
    pair = lax.rem(after, 2)
    block(pair, pair + 2, 8 + pair)
    for h, copy in enumerate(from_opposite):
        copy.wait_recv()
        begin, end = 2 * h, 2 * h + 2
        ready(opposite, begin, end)
        block(after, opposite, 4 + after, begin, end)
        block(opposite, before, 4 + opposite, begin, end)
        block(opposite, opposite, opposite, begin, end)
        pair = lax.rem(x, 2)
        block(pair, pair + 2, 8 + pair, begin, end)

    count = half.shape[0] // 2
    for copy, slot in zip(swaps, held):
        copy.wait_recv()
        here = pl.ds(slot * part, part)
        acc[here, :] = half[pl.ds(slot * rows + core * part, part), :] + near[here, :]

    size = count // 16
    me = x * 4 + y
    arrivals = []
    for i, (a, b) in enumerate(plane):
        to = lax.rem(x + a, 4) * 4 + lax.rem(y + b, 4)
        arrivals.append(send(
            acc.at[pl.ds(to * size, size)], slots.at[me],
            plane_send.at[i], plane_recv.at[i], at(a, 2 * b, 0),
        ))
    slots[me] = acc[pl.ds(me * size, size), :]
    for copy in arrivals:
        copy.wait_recv()
    zq, zr = z // 4, lax.rem(z, 4)
    total = slots[0]
    for i in range(1, 16):
        total += slots[i]

    for index, (ref, own_slot, steps) in enumerate(((quad, zq, (8, 4, 12)), (fours, zr, (2, 1, 15)))):
        ref[own_slot] = total
        arrivals = [
            send(
                ref.at[own_slot], ref.at[own_slot],
                z_send.at[3 * index + i], z_recv.at[3 * index + i], at(0, 0, d),
            )
            for i, d in enumerate(steps)
        ]
        for copy in arrivals:
            copy.wait_recv()
        total = ((ref[0] + ref[1]) + ref[2]) + ref[3]

    here = pl.ds(me * size, size)
    full[core, here, :] = total
    arrivals = [
        send(
            full.at[core, here], full.at[core, here],
            back_send.at[i], back_recv.at[i], at(a, 2 * b, 0),
        )
        for i, (a, b) in enumerate(plane)
    ]
    swaps = []
    for i, a in enumerate((0, 1, 3, 2)):
        for copy, (da, _) in zip(arrivals, plane):
            if da == (4 - a) % 4:
                copy.wait_recv()
        group = pl.ds(lax.rem(x + a, 4) * 4 * size, 4 * size)
        swaps.append(send(
            full.at[core, group], full.at[core, group],
            core_send.at[10 + i], core_recv.at[10 + i], other_core,
        ))
    for copy in swaps:
        copy.wait_recv()
    pairs = [(p, p, p) for p in range(4)] + [(p, (p + 1) % 4, 4 + p) for p in range(4)]
    pairs += [(p, p + 2, 8 + p) for p in range(2)]
    for a, b, slot in pairs:
        piece = full[:, part * slot:part * slot + part, :].reshape(rows, rows) * scale
        for p, q, value in ((a, b, piece),) if a == b else ((a, b, piece), (b, a, piece.T)):
            for ref, term in zip((gram, gram_mid, gram_low), split(value)):
                ref[rows * p:rows * p + rows, rows * q:rows * q + rows] = term

    first.wait()
    work_ref[...] = times(split(work_ref[...]), gram[...], gram_mid[...], gram_low[...])

    def step(i, carry):
        work = work_ref[...]
        inverse = chol_inverse(dot_nt(work, work))
        ahead = times(split(work), gram[...], gram_mid[...], gram_low[...])
        work_ref[...] = wide_times(inverse, jnp.where(i < iters - 1, ahead, work))
        return carry

    lax.fori_loop(0, iters, step, 0)

    parts = split(work_ref[...])
    ranks = work_ref.shape[0]
    share = ranks // 4
    flat_out = proj.reshape(ranks * 8, 128)
    arrivals = []
    for h in range(2):
        wide = slice(512 * h, 512 * h + 512)
        result = times(parts, high[:, wide], mid[:, wide], low[:, wide])
        for s in range(4):
            flat_out[pl.ds(4 * h + s, ranks, stride=8), :] = result[:, 128 * s:128 * s + 128]
        for k, d in enumerate((2, 1, 3)):
            arrivals.append(send(
                proj.at[pl.ds(lax.rem(x + d, 4) * share, share), pl.ds(4 * h, 4), :],
                out_ref.at[:, pl.ds(x * 8 + 4 * h, 4), :],
                out_send.at[h, k], out_recv.at[h, k], at(d, 0, 0),
            ))
    out_ref[:, pl.ds(x * 8, 8), :] = proj[pl.ds(x * share, share)]
    for copy in arrivals:
        copy.wait_recv()
    for copy in sends:
        copy.wait_send()


def per_device(field, start):
    ncols = field.shape[1] * field.shape[2] * lax.axis_size("ga") * lax.axis_size("ha")
    rows = field.shape[0]
    total, ranks = start.shape
    dma, vmem, f32 = pltpu.SemaphoreType.DMA, pltpu.VMEM, jnp.float32
    piece = 5 * rows // 16
    return pl.pallas_call(
        functools.partial(step_kernel, ITERS, 1.0 / ncols),
        out_shape=jax.ShapeDtypeStruct((ranks // 4, 32, 128), f32),
        in_specs=[pl.BlockSpec(memory_space=pltpu.HBM)] * 2,
        out_specs=pl.BlockSpec(memory_space=vmem),
        scratch_shapes=[
            vmem((total, 8, 128), f32),
            vmem((total, 1024), jnp.bfloat16),
            vmem((total, 1024), jnp.bfloat16),
            vmem((total, 1024), jnp.bfloat16),
            vmem((10 * rows, rows), f32),
            vmem((5 * rows, rows), f32),
            vmem((5 * rows, rows), f32),
            vmem((16, piece, rows), f32),
            vmem((4, piece, rows), f32),
            vmem((4, piece, rows), f32),
            vmem((2, 5 * rows, rows), f32),
            vmem((total, total), jnp.bfloat16),
            vmem((total, total), jnp.bfloat16),
            vmem((total, total), jnp.bfloat16),
            vmem((ranks, total), f32),
            vmem((ranks, 8, 128), f32),
            dma((6,)), dma((6,)), dma(()), dma(()), dma((14,)), dma((14,)), dma((15,)), dma((15,)),
            dma((6,)), dma((6,)), dma((15,)), dma((15,)), dma((2, 3)), dma((2, 3)),
            pltpu.SemaphoreType.REGULAR((9,)),
        ],
        compiler_params=pltpu.CompilerParams(
            collective_id=0, has_side_effects=True, vmem_limit_bytes=VMEM_LIMIT
        ),
        name="hosvd_step",
    )(
        pltpu.with_memory_space_constraint(field, pltpu.HBM),
        pltpu.with_memory_space_constraint(start.T, pltpu.HBM),
    )


def solution(mesh):
    placed = (P("af", "ga", "ha"), P())
    return jax.shard_map(
        per_device, mesh=mesh, in_specs=placed, out_specs=P("af", "ga", "ha"), check_vma=False
    )
```

```python
import functools

import jax
import jax.numpy as jnp
from jax import lax
from jax.experimental import pallas as pl
from jax.experimental.pallas import tpu as pltpu
from jax.sharding import PartitionSpec as P

ITERS = 6
HIGHEST = lax.Precision.HIGHEST
MESH = pl.DeviceIdType.MESH
NT = (((1,), (1,)), ((), ()))
VMEM_LIMIT = 32 * 2**20


def dot_nt(a, b):
    return lax.dot_general(a, b, NT, precision=HIGHEST, preferred_element_type=jnp.float32)


def dot16(a, b):
    return jnp.dot(a, b, preferred_element_type=jnp.float32)


def dot16_nt(a, b):
    return lax.dot_general(a, b, NT, preferred_element_type=jnp.float32)


def split(x):
    high = x.astype(jnp.bfloat16)
    rest = x - high.astype(jnp.float32)
    mid = rest.astype(jnp.bfloat16)
    low = (rest - mid.astype(jnp.float32)).astype(jnp.bfloat16)
    return high, mid, low


def times(parts, high, mid, low):
    n = parts[0].shape[0]
    first = dot16(jnp.concatenate(parts, axis=0), high)
    second = dot16(jnp.concatenate(parts[:2], axis=0), mid)
    third = dot16(parts[0], low)
    return first[:n] + (
        (first[n:2 * n] + second[:n]) + (second[n:] + (first[2 * n:] + third))
    )


def wide_times(a, b):
    ah, am, al = split(a)
    zero = jnp.zeros(b.shape, jnp.bfloat16)
    bh, bm, bl = (jnp.concatenate([zero, term], axis=0) for term in split(b))
    left = jnp.concatenate([ah, ah, ah, am, am, al], axis=1)
    return dot16(left, jnp.concatenate([bh, bm, bl, bh, bm, bh], axis=0))


def chol_inverse(inner):
    n = inner.shape[0]
    panels = n // 8
    full = (8, 2 * n)
    sub = lax.broadcasted_iota(jnp.int32, full, 0)
    lane = lax.broadcasted_iota(jnp.int32, full, 1)
    rows = []
    for m in range(panels):
        eye = jnp.where(lane[:, :n] == sub[:, :n] + 8 * m, 1.0, 0.0).astype(jnp.float32)
        rows.append(jnp.concatenate([inner[8 * m:8 * m + 8, :], eye], axis=1))

    def over_lanes(m, j):
        return jnp.broadcast_to(rows[m][:, j:j + 1], full)

    def over_rows(value, q):
        return jnp.broadcast_to(value[q:q + 1, :], full)

    out = []
    ahead = {m: [over_lanes(m, p) for p in range(8)] for m in range(2)}
    for k in range(panels):
        later = range(k + 1, panels)
        cols = dict(ahead)
        for m in later:
            if m not in cols:
                cols[m] = [over_lanes(m, 8 * k + p) for p in range(8)]
        early = {
            m: [over_lanes(m, 8 * (k + 1) + j) for j in range(8)]
            for m in range(k + 1, min(k + 3, panels))
        }
        row = [over_rows(rows[k], p) for p in range(8)]
        diag = {(q, p): over_rows(cols[k][p], q) for p in range(8) for q in range(p, 8)}
        inv = []
        for p in range(8):
            inv.append(1.0 / diag[p, p])
            for q in range(p + 1, 8):
                factor = diag[q, p] * inv[p]
                for r in range(p + 1, q + 1):
                    diag[q, r] = diag[q, r] - factor * diag[r, p]
                row[q] = row[q] - factor * row[p]
                for m in later:
                    cols[m][q] = cols[m][q] - factor * cols[m][p]
        scaled = {m: [cols[m][p] * inv[p] for p in range(8)] for m in later}
        ahead = {}
        if k + 1 < panels:
            spread = [[over_rows(cols[k + 1][p], j) for p in range(8)] for j in range(8)]
            for m in early:
                ahead[m] = []
                for j in range(8):
                    value = early[m][j]
                    for p in range(8):
                        value = value - scaled[m][p] * spread[j][p]
                    ahead[m].append(value)
        for m in later:
            terms = [scaled[m][p] * row[p] for p in range(8)]
            while len(terms) > 1:
                terms = [terms[i] + terms[i + 1] for i in range(0, len(terms), 2)]
            rows[m] = rows[m] - terms[0]
        done = row[0] * lax.rsqrt(diag[0, 0])
        for p in range(1, 8):
            done = jnp.where(sub == p, row[p] * lax.rsqrt(diag[p, p]), done)
        out.append(jnp.where(lane >= n, done, 0.0))
    return jnp.concatenate(out, axis=0)


def step_kernel(iters, scale, field_ref, start_ref, out_ref, cols, high, mid, low, half, near, acc,
                slots, quad, fours, full, gram, gram_mid, gram_low, work_ref, proj, in_send, in_recv, own_sem, start_sem,
                core_send, core_recv, plane_send, plane_recv, z_send, z_recv, back_send, back_recv,
                out_send, out_recv, met):
    x, g, z = lax.axis_index("af"), lax.axis_index("ga"), lax.axis_index("ha")
    core = lax.rem(g, 2)
    y = g // 2
    rows = field_ref.shape[0]

    def at(dx, dg, dz):
        return {"af": lax.rem(x + dx, 4), "ga": lax.rem(g + dg, 8), "ha": lax.rem(z + dz, 16)}

    other_core = {"af": x, "ga": g + 1 - 2 * core, "ha": z}
    plane = [
        (2, 2), (1, 2), (3, 2), (2, 1), (2, 3), (1, 1), (1, 3), (3, 1), (3, 3),
        (2, 0), (0, 2), (1, 0), (3, 0), (0, 1), (0, 3),
    ]
    sends = []

    def send(src, dst, send_sem, recv_sem, device):
        copy = pltpu.make_async_remote_copy(
            src_ref=src, dst_ref=dst, send_sem=send_sem, recv_sem=recv_sem,
            device_id=device, device_id_type=MESH,
        )
        copy.start()
        sends.append(copy)
        return copy

    barrier = pltpu.get_barrier_semaphore()
    nearest = [at(1, 0, 0), at(3, 0, 0), at(2, 0, 0), other_core]
    nearest += [at(0, 2, 0), at(0, 6, 0), at(0, 0, 1), at(0, 0, 15)]
    for device in nearest:
        pl.semaphore_signal(barrier, inc=1, device_id=device, device_id_type=MESH)
    pl.semaphore_wait(barrier, len(nearest))

    for k, d in enumerate((1, 3)):
        send(
            field_ref.at[:, pl.ds(lax.rem(x + d, 4) * 8, 8), :], cols.at[pl.ds(x * rows, rows)],
            in_send.at[k], in_recv.at[k], at(d, 0, 0),
        )
    from_before, from_after = sends

    def send_opposite():
        to = lax.rem(x + 2, 4)
        return [
            send(
                field_ref.at[:, pl.ds(to * 8 + 2 * h, 2), :],
                cols.at[pl.ds(x * rows, rows), pl.ds(2 * h, 2), :],
                in_send.at[2 + h], in_recv.at[2 + h], at(2, 0, 0),
            )
            for h in range(4)
        ]

    from_opposite = send_opposite()
    own = pltpu.make_async_copy(
        field_ref.at[:, pl.ds(x * 8, 8), :], cols.at[pl.ds(x * rows, rows)], own_sem
    )
    own.start()
    first = pltpu.make_async_copy(start_ref, work_ref, start_sem)
    first.start()

    rounds = (
        (at(0, 2, 0), at(0, 6, 0), at(0, 0, 1), at(0, 0, 15)),
        (at(0, 4, 0), at(0, 0, 2), at(0, 0, 14)),
        (at(0, 0, 4), at(0, 0, 12)),
    )
    index = 0
    for turn, devices in enumerate(rounds):
        for i, device in enumerate(devices):
            pl.semaphore_signal(met.at[index + i], inc=1, device_id=device, device_id_type=MESH)
        for i in range(len(devices)):
            pl.semaphore_wait(met.at[index + i], 1)
        index += len(devices)

    flat = cols.reshape(4 * rows * 8, 128)

    def ready(p, start=0, stop=8):
        for s in range(start, stop):
            parts = split(flat[pl.ds(p * rows * 8 + s, rows, stride=8), :])
            for ref, part in zip((high, mid, low), parts):
                ref[pl.ds(p * rows, rows), 128 * s:128 * s + 128] = part

    part = rows // 2
    swaps, held = [], []

    def block(p, q, slot, begin=0, end=8):
        left, right = pl.ds(p * rows, rows), pl.ds(q * rows, rows)
        wide = slice(128 * begin, 128 * end)
        main = dot16_nt(
            jnp.concatenate([high[left, wide], mid[left, wide]], axis=0),
            jnp.concatenate([high[right, wide], mid[right, wide]], axis=0),
        )
        small = dot16_nt(low[left, wide], high[right, wide])
        small += dot16_nt(high[left, wide], low[right, wide]) + main[rows:, rows:]
        total = main[:rows, :rows] + ((main[:rows, rows:] + main[rows:, :rows]) + small)
        whole = pl.ds(slot * rows, rows)
        half[whole, :] = total if begin == 0 else half[whole, :] + total
        if end < 8:
            return
        theirs = pl.ds(slot * rows + (1 - core) * part, part)
        index = len(swaps)
        swaps.append(send(
            half.at[theirs], near.at[pl.ds(slot * part, part)],
            core_send.at[index], core_recv.at[index], other_core,
        ))
        held.append(slot)

    after, opposite, before = (lax.rem(x + d, 4) for d in (1, 2, 3))
    own.wait()
    ready(x)
    block(x, x, x)
    from_after.wait_recv()
    ready(after)
    block(x, after, 4 + x)
    block(after, after, after)
    from_before.wait_recv()
    ready(before)
    block(before, x, 4 + before)
    block(before, before, before)
    pair = lax.rem(after, 2)
    block(pair, pair + 2, 8 + pair)
    for h, copy in enumerate(from_opposite):
        copy.wait_recv()
        begin, end = 2 * h, 2 * h + 2
        ready(opposite, begin, end)
        block(after, opposite, 4 + after, begin, end)
        block(opposite, before, 4 + opposite, begin, end)
        block(opposite, opposite, opposite, begin, end)
        pair = lax.rem(x, 2)
        block(pair, pair + 2, 8 + pair, begin, end)

    count = half.shape[0] // 2
    for copy, slot in zip(swaps, held):
        copy.wait_recv()
        here = pl.ds(slot * part, part)
        acc[here, :] = half[pl.ds(slot * rows + core * part, part), :] + near[here, :]

    size = count // 16
    me = x * 4 + y
    arrivals = []
    for i, (a, b) in enumerate(plane):
        to = lax.rem(x + a, 4) * 4 + lax.rem(y + b, 4)
        arrivals.append(send(
            acc.at[pl.ds(to * size, size)], slots.at[me],
            plane_send.at[i], plane_recv.at[i], at(a, 2 * b, 0),
        ))
    slots[me] = acc[pl.ds(me * size, size), :]
    for copy in arrivals:
        copy.wait_recv()
    zq, zr = z // 4, lax.rem(z, 4)
    total = slots[0]
    for i in range(1, 16):
        total += slots[i]

    for index, (ref, own_slot, steps) in enumerate(((quad, zq, (8, 4, 12)), (fours, zr, (2, 1, 15)))):
        ref[own_slot] = total
        arrivals = [
            send(
                ref.at[own_slot], ref.at[own_slot],
                z_send.at[3 * index + i], z_recv.at[3 * index + i], at(0, 0, d),
            )
            for i, d in enumerate(steps)
        ]
        for copy in arrivals:
            copy.wait_recv()
        total = ((ref[0] + ref[1]) + ref[2]) + ref[3]

    here = pl.ds(me * size, size)
    full[core, here, :] = total
    arrivals = [
        send(
            full.at[core, here], full.at[core, here],
            back_send.at[i], back_recv.at[i], at(a, 2 * b, 0),
        )
        for i, (a, b) in enumerate(plane)
    ]
    swaps = []

    def forward(group):
        index = 10 + len(swaps)
        swaps.append(send(
            full.at[core, group], full.at[core, group],
            core_send.at[index], core_recv.at[index], other_core,
        ))

    for a in (0, 1, 3):
        for copy, (da, _) in zip(arrivals, plane):
            if da == (4 - a) % 4:
                copy.wait_recv()
        forward(pl.ds(lax.rem(x + a, 4) * 4 * size, 4 * size))
    for b in (0, 1, 3, 2):
        arrivals[plane.index((2, b))].wait_recv()
        forward(pl.ds((lax.rem(x + 2, 4) * 4 + lax.rem(y + 4 - b, 4)) * size, size))
    for copy in swaps:
        copy.wait_recv()
    pairs = [(p, p, p) for p in range(4)] + [(p, (p + 1) % 4, 4 + p) for p in range(4)]
    pairs += [(p, p + 2, 8 + p) for p in range(2)]
    for a, b, slot in pairs:
        piece = full[:, part * slot:part * slot + part, :].reshape(rows, rows) * scale
        for p, q, value in ((a, b, piece),) if a == b else ((a, b, piece), (b, a, piece.T)):
            for ref, term in zip((gram, gram_mid, gram_low), split(value)):
                ref[rows * p:rows * p + rows, rows * q:rows * q + rows] = term

    first.wait()
    work_ref[...] = times(split(work_ref[...]), gram[...], gram_mid[...], gram_low[...])

    def step(i, carry):
        work = work_ref[...]
        inverse = chol_inverse(dot_nt(work, work))
        ahead = times(split(work), gram[...], gram_mid[...], gram_low[...])
        work_ref[...] = wide_times(inverse, jnp.where(i < iters - 1, ahead, work))
        return carry

    lax.fori_loop(0, iters, step, 0)

    parts = split(work_ref[...])
    ranks = work_ref.shape[0]
    share = ranks // 4
    flat_out = proj.reshape(ranks * 8, 128)
    arrivals = []
    for h in range(2):
        wide = slice(512 * h, 512 * h + 512)
        result = times(parts, high[:, wide], mid[:, wide], low[:, wide])
        for s in range(4):
            flat_out[pl.ds(4 * h + s, ranks, stride=8), :] = result[:, 128 * s:128 * s + 128]
        for k, d in enumerate((2, 1, 3)):
            arrivals.append(send(
                proj.at[pl.ds(lax.rem(x + d, 4) * share, share), pl.ds(4 * h, 4), :],
                out_ref.at[:, pl.ds(x * 8 + 4 * h, 4), :],
                out_send.at[h, k], out_recv.at[h, k], at(d, 0, 0),
            ))
    out_ref[:, pl.ds(x * 8, 8), :] = proj[pl.ds(x * share, share)]
    for copy in arrivals:
        copy.wait_recv()
    for copy in sends:
        copy.wait_send()


def per_device(field, start):
    ncols = field.shape[1] * field.shape[2] * lax.axis_size("ga") * lax.axis_size("ha")
    rows = field.shape[0]
    total, ranks = start.shape
    dma, vmem, f32 = pltpu.SemaphoreType.DMA, pltpu.VMEM, jnp.float32
    piece = 5 * rows // 16
    return pl.pallas_call(
        functools.partial(step_kernel, ITERS, 1.0 / ncols),
        out_shape=jax.ShapeDtypeStruct((ranks // 4, 32, 128), f32),
        in_specs=[pl.BlockSpec(memory_space=pltpu.HBM)] * 2,
        out_specs=pl.BlockSpec(memory_space=vmem),
        scratch_shapes=[
            vmem((total, 8, 128), f32),
            vmem((total, 1024), jnp.bfloat16),
            vmem((total, 1024), jnp.bfloat16),
            vmem((total, 1024), jnp.bfloat16),
            vmem((10 * rows, rows), f32),
            vmem((5 * rows, rows), f32),
            vmem((5 * rows, rows), f32),
            vmem((16, piece, rows), f32),
            vmem((4, piece, rows), f32),
            vmem((4, piece, rows), f32),
            vmem((2, 5 * rows, rows), f32),
            vmem((total, total), jnp.bfloat16),
            vmem((total, total), jnp.bfloat16),
            vmem((total, total), jnp.bfloat16),
            vmem((ranks, total), f32),
            vmem((ranks, 8, 128), f32),
            dma((6,)), dma((6,)), dma(()), dma(()), dma((17,)), dma((17,)), dma((15,)), dma((15,)),
            dma((6,)), dma((6,)), dma((15,)), dma((15,)), dma((2, 3)), dma((2, 3)),
            pltpu.SemaphoreType.REGULAR((9,)),
        ],
        compiler_params=pltpu.CompilerParams(
            collective_id=0, has_side_effects=True, vmem_limit_bytes=VMEM_LIMIT
        ),
        name="hosvd_step",
    )(
        pltpu.with_memory_space_constraint(field, pltpu.HBM),
        pltpu.with_memory_space_constraint(start.T, pltpu.HBM),
    )


def solution(mesh):
    placed = (P("af", "ga", "ha"), P())
    return jax.shard_map(
        per_device, mesh=mesh, in_specs=placed, out_specs=P("af", "ga", "ha"), check_vma=False
    )
```
